128 devices in a mesh: samp: 16 (over z_hi, x, core), blk: 8 (over z_lo, y).
Axes of the slice: x: 4, y: 4, z: 4 (z_hi: 2, z_lo: 2; z = z_hi * 2 + z_lo), core: 2. Of those that a mesh axis runs over, the one named last changes fastest.
Arguments:
- genotypes: int32 [32768, 12288], P('samp', 'blk'), may hold values from 0 to 2
- phenotype: float32 [32768], P('samp'), may hold values from -15 to 15
- fold_ids: int32 [32768], P('samp'), may hold values from 0 to 4, as said below
Outputs:
- coeff_all: float32 [12288, 400], P('blk')
- fold_scores: float32 [2, 400], replicated
The draws below stay inside these ranges and needn't reach their ends.
Inputs may be any that keep to these rules, and one draw needn't show every extreme that they name: `fold_ids`: every fold holds 6553 or 6554 people.
All inputs are finite; a program needn't handle non-finite values.
Results may differ from the reference program's by a relative error of at most 0.0003.
Values sent between devices are 32-bit elements; how exact they have to be, the bound alone decides.
No kernel may reach another device: no remote copies, remote signals or barrier semaphores. Data moves between devices by JAX's collectives and lax.ppermute only.
A program may use at most 128 MiB of HBM per device.

```python
import math
import jax
import jax.numpy as jnp
from jax import lax

BLOCK = 1536
FOLDS = 5
LAMBDAS = 20
SWEEPS = 3
GRID = 400
NSAMP = 32768
NSNP = 12288


def draw_genotypes(key, part):
    freq_key, first_key, second_key = jax.random.split(key, 3)
    frequency = jax.random.randint(freq_key, (NSNP,), 51, 513, dtype=jnp.int32)
    first_copy = jax.random.randint(first_key, (NSAMP, NSNP), 0, 1024, dtype=jnp.int32) < frequency[None, :]
    second_copy = jax.random.randint(second_key, (NSAMP, NSNP), 0, 1024, dtype=jnp.int32) < frequency[None, :]
    return first_copy.astype(jnp.int32) + second_copy.astype(jnp.int32)


def draw_phenotype(key, part):
    row_scale = 1.0 + 2.0 * jnp.arange(NSAMP, dtype=jnp.float32) / (NSAMP - 1)
    normal_part = jnp.clip(jax.random.normal(key, (NSAMP,), jnp.float32), -5.0, 5.0)
    return (normal_part * row_scale).astype(jnp.float32)


def draw_fold_ids(key, part):
    return (jax.random.permutation(key, NSAMP) % FOLDS).astype(jnp.int32)


def setup_inputs(seed: int = 0) -> dict:
    key_of = jax.random.split(jax.random.key(seed), 4)
    return {
        "genotypes": draw_genotypes(jax.random.fold_in(key_of[3], 71), 0),
        "phenotype": draw_phenotype(jax.random.fold_in(key_of[3], 71), 0),
        "fold_ids": draw_fold_ids(jax.random.fold_in(key_of[3], 71), 0),
    }


step_size = 0.6
epsilon = 1e-05
lambda_base = 0.1
lambda_ratio = 1.2
shrink_unit = 0.2
highest = lax.Precision.HIGHEST

def grid_tables():
    column = jnp.arange(GRID)
    fold_of = column % FOLDS
    levels = column // FOLDS % LAMBDAS
    penalty = lambda_base * jnp.exp(levels.astype(jnp.float32) * math.log(lambda_ratio))
    shrink = shrink_unit * (column // (FOLDS * LAMBDAS) + 1).astype(jnp.float32)
    return (fold_of, penalty, shrink)

def soft_threshold(values, cutoff):
    return values - jnp.clip(values, -cutoff, cutoff)

def reference(genotypes, phenotype, fold_ids):
    sample_count = genotypes.shape[0]
    snp_total = genotypes.shape[1]
    dosage = genotypes.astype(jnp.float32)
    onehot = fold_ids[:, None] == jnp.arange(FOLDS)[None, :]
    pheno_split = jnp.where(onehot, phenotype[:, None], 0.0).astype(jnp.float32)
    geno_sum = lax.optimization_barrier(jnp.sum(genotypes, axis=0)).astype(jnp.float32)
    geno_sq = lax.optimization_barrier(jnp.sum(genotypes * genotypes, axis=0)).astype(jnp.float32)
    fold_count = lax.optimization_barrier(jnp.sum(onehot.astype(jnp.int32), axis=0)).astype(jnp.float32)
    fold_pheno_sum = lax.optimization_barrier(jnp.sum(pheno_split, axis=0))
    geno_pheno = jnp.dot(pheno_split.T, dosage, precision=highest)
    snp_mean = geno_sum / sample_count
    scales = jnp.sqrt(geno_sq / sample_count - snp_mean * snp_mean + epsilon)
    train_geno = lax.optimization_barrier(jnp.sum(geno_pheno, axis=0))[None, :] - geno_pheno
    train_pheno = jnp.sum(fold_pheno_sum) - fold_pheno_sum
    zscore = (train_geno - train_pheno[:, None] * snp_mean[None, :]) / (scales[None, :] * jnp.sqrt(sample_count - fold_count)[:, None])
    fold_of, penalty, shrink = grid_tables()
    target_all = zscore.T[:, fold_of]
    predicted = jnp.zeros((sample_count, GRID), jnp.float32)
    coeff_list = []
    for block_idx in range(snp_total // BLOCK):
        low_col = block_idx * BLOCK
        dose_block = dosage[:, low_col:low_col + BLOCK]
        gram_sum = jnp.dot(dose_block.T, dose_block, precision=highest)
        mean_block = snp_mean[low_col:low_col + BLOCK]
        scale_block = scales[low_col:low_col + BLOCK]
        ld_block = (gram_sum / sample_count - mean_block[:, None] * mean_block[None, :]) / (scale_block[:, None] * scale_block[None, :])
        target = target_all[low_col:low_col + BLOCK]
        coeffs = jnp.zeros((BLOCK, GRID), jnp.float32)
        for sweep_idx in range(SWEEPS):
            gradient = (1.0 - shrink) * jnp.dot(ld_block, coeffs, precision=highest) + shrink * coeffs - target
            coeffs = soft_threshold(coeffs - step_size * gradient, step_size * penalty)
        weighted = lax.optimization_barrier((coeffs / scale_block[:, None]).astype(jnp.bfloat16)).astype(jnp.float32)
        predicted = predicted + (jnp.dot(dose_block, weighted, precision=highest) - jnp.dot(mean_block[None, :], weighted, precision=highest))
        coeff_list.append(coeffs)
    predicted = predicted / math.sqrt(snp_total)
    chosen = fold_ids[:, None] == fold_of[None, :]
    numerator = lax.optimization_barrier(jnp.sum(jnp.where(chosen, predicted * phenotype[:, None], 0.0), axis=0))
    denominator = lax.optimization_barrier(jnp.sum(jnp.where(chosen, predicted * predicted, 0.0), axis=0))
    counts = fold_count[fold_of]
    fold_scores = jnp.stack([numerator / counts, denominator / counts])
    return (jnp.concatenate(coeff_list, axis=0), fold_scores)
```

```python
import math

import jax
import jax.numpy as jnp
from jax import lax
from jax.sharding import PartitionSpec as P

FOLDS = 5
LAMBDAS = 20
GRID = 400
BASE = FOLDS * LAMBDAS
SHRINKS = GRID // BASE

step_size = 0.6
epsilon = 1e-05
lambda_base = 0.1
lambda_ratio = 1.2
shrink_unit = 0.2


def soft_threshold(values, cutoff):
    return values - jnp.clip(values, -cutoff, cutoff)


def swap(values, axis, bit):
    size = lax.axis_size(axis)
    return lax.ppermute(values, axis, [(i, i ^ bit) for i in range(size)])


def rounded(values):
    return lax.reduce_precision(values, 8, 7)


def split2(values):
    high = rounded(values)
    return high.astype(jnp.bfloat16), (values - high).astype(jnp.bfloat16)


def split3(values):
    high = rounded(values)
    return (high.astype(jnp.bfloat16),) + split2(values - high)


def order4(parts, place):
    low, high = (place & 1) == 1, (place & 2) == 2
    a, b, c, d = parts
    a, b, c, d = (jnp.where(low, b, a), jnp.where(low, a, b), jnp.where(low, d, c), jnp.where(low, c, d))
    return jnp.where(high, c, a), jnp.where(high, d, b), jnp.where(high, a, c), jnp.where(high, b, d)


def reduce_scatter(values, core, place):
    half = values.shape[0] // 2
    width = values.shape[1] // 4
    kept = lax.dynamic_slice_in_dim(values, core * half, half, 0)
    sent = lax.dynamic_slice_in_dim(values, (1 - core) * half, half, 0)
    kept = kept + swap(sent, "samp", 1)
    kept = kept + swap(kept, "samp", 8)
    got = [
        swap(lax.dynamic_slice_in_dim(kept, (place ^ k) * width, width, 1), "samp", 2 * k) for k in (1, 2, 3)
    ]
    mine = lax.dynamic_slice_in_dim(kept, place * width, width, 1)
    return mine + got[0] + got[1] + got[2]


def gather(piece, core, place):
    parts = [piece] + [swap(piece, "samp", 2 * k) for k in (1, 2, 3)]
    half = jnp.concatenate(order4(parts, place), axis=1)
    other = swap(half, "samp", 1)
    first = core == 0
    return jnp.concatenate([jnp.where(first, half, other), jnp.where(first, other, half)], axis=0)


def all_sum(values, bits):
    for axis, group in bits:
        got = [swap(values, axis, bit) for bit in group]
        values = values + got[0] if len(got) == 1 else (values + got[0]) + (got[1] + got[2])
    return values


SAMP_BITS = (("samp", (1,)), ("samp", (8,)), ("samp", (2, 4, 6)))


def by_fold(table, rows):
    fold_of = lax.broadcasted_iota(jnp.int32, (rows, 1), 0) % FOLDS
    out = jnp.zeros((rows, table.shape[1]), table.dtype)
    for fold in range(FOLDS):
        out = jnp.where(fold_of == fold, table[fold : fold + 1], out)
    return out


def people_times(coeff, dosage, offset):
    rows = coeff.shape[0]
    both = jnp.concatenate(split2(coeff), axis=0)
    out = lax.dot_general(both, dosage, (((1,), (1,)), ((), ())), preferred_element_type=jnp.float32)
    return out[:rows] + out[rows:] - offset


def snps_times(scores, dosage):
    rows = scores.shape[0]
    both = jnp.concatenate(split2(scores), axis=0)
    out = lax.dot_general(both, dosage, (((1,), (0,)), ((), ())), preferred_element_type=jnp.float32)
    return out[:rows] + out[rows:]


def local(genotypes, phenotype, fold_ids):
    num_rows, block_width = genotypes.shape
    sample_count = num_rows * lax.axis_size("samp")
    snp_total = block_width * lax.axis_size("blk")
    samp = lax.axis_index("samp")
    core, place = samp % 2, samp // 2 % 4
    dosage = genotypes.astype(jnp.bfloat16)

    onehot = fold_ids[None, :] == jnp.arange(FOLDS)[:, None]
    pheno_split = jnp.where(onehot, phenotype[None, :], 0.0)
    left = jnp.concatenate(split3(pheno_split), axis=0)
    parts = lax.dot_general(left, dosage, (((1,), (0,)), ((), ())), preferred_element_type=jnp.float32)
    geno_pheno = parts[:5] + parts[5:10] + parts[10:15]
    geno_sum = jnp.sum(genotypes, axis=0).astype(jnp.float32)
    geno_sq = jnp.sum(genotypes * genotypes, axis=0).astype(jnp.float32)
    counts = jnp.sum(onehot.astype(jnp.float32), axis=1)
    fold_sum = jnp.sum(pheno_split, axis=1)
    extra = jnp.concatenate([counts, fold_sum, jnp.zeros((block_width - 10,), jnp.float32)])
    stats = jnp.concatenate([geno_pheno, geno_sum[None], geno_sq[None], extra[None]], axis=0)
    stats = all_sum(stats, SAMP_BITS)
    geno_pheno = stats[:5]
    fold_count = stats[7, :5][:, None]
    fold_pheno_sum = stats[7, 5:10][:, None]
    snp_mean = stats[5:6] / sample_count
    scales = jnp.sqrt(stats[6:7] / sample_count - snp_mean * snp_mean + epsilon)
    train_geno = jnp.sum(geno_pheno, axis=0, keepdims=True) - geno_pheno
    train_pheno = jnp.sum(fold_pheno_sum) - fold_pheno_sum
    zscore = (train_geno - train_pheno * snp_mean) / (scales * jnp.sqrt(sample_count - fold_count))
    inverse = 1.0 / scales

    level = (lax.broadcasted_iota(jnp.int32, (BASE, 1), 0) // FOLDS).astype(jnp.float32)
    cutoff = step_size * (lambda_base * jnp.exp(level * math.log(lambda_ratio)))
    target = by_fold(zscore, BASE)
    coeff0 = soft_threshold(step_size * target, cutoff)

    def centred(coeff):
        scaled = coeff * inverse
        offset = jnp.sum(scaled * snp_mean, axis=1, keepdims=True)
        return scaled, offset

    scaled, offset = centred(coeff0)
    scores = people_times(scaled, dosage, offset)
    product = reduce_scatter(snps_times(scores, dosage), core, place)
    product = gather(product, core, place) * (inverse / sample_count)

    def sweep(coeff, product, target, shrink, cutoff):
        gradient = (1.0 - shrink) * product + shrink * coeff - target
        return soft_threshold(coeff - step_size * gradient, cutoff)

    shrinks = [shrink_unit * (group + 1) for group in range(SHRINKS)]
    coeff1 = jnp.concatenate([sweep(coeff0, product, target, shrink, cutoff) for shrink in shrinks], axis=0)
    scaled, offset = centred(coeff1)
    scores = people_times(scaled, dosage, offset)
    piece = reduce_scatter(snps_times(scores, dosage), core, place)

    half, width = GRID // 2, block_width // 4
    here = lambda a: lax.dynamic_slice_in_dim(a, place * width, width, 1)
    column = core * half + lax.broadcasted_iota(jnp.int32, (half, 1), 0)
    shrink = shrink_unit * (column // BASE + 1).astype(jnp.float32)
    level = (column // FOLDS % LAMBDAS).astype(jnp.float32)
    cutoff2 = step_size * (lambda_base * jnp.exp(level * math.log(lambda_ratio)))
    coeff_piece = lax.dynamic_slice(coeff1, (core * half, place * width), (half, width))
    target_piece = by_fold(here(zscore), half)
    piece = sweep(coeff_piece, piece * (here(inverse) / sample_count), target_piece, shrink, cutoff2)
    coeff_all = gather(piece, core, place)

    wide = rounded(coeff_all / scales)
    weighted = wide.astype(jnp.bfloat16)
    offset = jnp.sum(wide * snp_mean, axis=1)
    centred_pheno = geno_pheno - snp_mean * fold_pheno_sum
    numerator = jnp.sum(wide * by_fold(centred_pheno, GRID), axis=1)
    grouped = weighted.reshape(GRID // FOLDS, FOLDS, block_width).transpose(1, 0, 2).reshape(GRID, block_width)
    offset = offset.reshape(GRID // FOLDS, FOLDS).T.reshape(GRID, 1)
    predicted = lax.dot_general(grouped, dosage, (((1,), (1,)), ((), ())), preferred_element_type=jnp.float32) - offset
    predicted = predicted.reshape(FOLDS, GRID // FOLDS, num_rows)
    predicted = jnp.sum(jnp.where(onehot[:, None, :], predicted, 0.0), axis=0)

    blk = lax.axis_index("blk")
    along = blk % 4
    width = num_rows // 4
    mine = lax.dynamic_slice_in_dim(predicted, along * width, width, 1)
    for k in (1, 2, 3):
        mine = mine + swap(lax.dynamic_slice_in_dim(predicted, (along ^ k) * width, width, 1), "blk", k)
    mine = mine + swap(mine, "blk", 4)
    numerator = numerator + swap(numerator, "blk", 4)
    folds_here = lax.dynamic_slice_in_dim(fold_ids, along * width, width, 0)
    square = mine * mine
    denominator = jnp.stack(
        [jnp.sum(jnp.where((folds_here == fold)[None, :], square, 0.0), axis=1) for fold in range(FOLDS)], axis=1
    ).reshape(GRID)
    sums = jnp.stack([numerator / lax.axis_size("samp"), denominator])
    sums = all_sum(sums, SAMP_BITS + (("blk", (1, 2, 3)),))
    count_of = by_fold(fold_count, GRID)[:, 0]
    fold_scores = jnp.stack([sums[0] / math.sqrt(snp_total), sums[1] / snp_total]) / count_of[None, :]
    return (coeff_all.T, fold_scores)


def solution(mesh):
    return jax.shard_map(
        local,
        mesh=mesh,
        in_specs=(P("samp", "blk"), P("samp"), P("samp")),
        out_specs=(P("blk", None), P()),
        check_vma=False,
    )
```

```python
import functools
import math

import jax
import jax.numpy as jnp
from jax import lax
from jax.experimental import pallas as pl
from jax.experimental.pallas import tpu as pltpu
from jax.sharding import PartitionSpec as P

FOLDS = 5
LAMBDAS = 20
GRID = 400
BASE = FOLDS * LAMBDAS
SHRINKS = GRID // BASE
LEVELS = GRID // FOLDS
ROWS0 = 112
ROWS1 = 104
PEOPLE = 32768
SNPS = 12288
VMEM = 56 * 1024 * 1024

step_size = 0.6
epsilon = 1e-05
lambda_base = 0.1
lambda_ratio = 1.2
shrink_unit = 0.2

NT = (((1,), (1,)), ((), ()))
NN = (((1,), (0,)), ((), ()))
TN = (((0,), (0,)), ((), ()))


def matmul(left, right, dims):
    return lax.dot_general(left, right, dims, preferred_element_type=jnp.float32)


def soft_threshold(values, cutoff):
    return values - jnp.clip(values, -cutoff, cutoff)


def swap(values, axis, bit):
    size = lax.axis_size(axis)
    return lax.ppermute(values, axis, [(i, i ^ bit) for i in range(size)])


def rounded(values):
    return lax.reduce_precision(values, 8, 7)


def split2(values):
    high = values.astype(jnp.bfloat16)
    return high, (values - high.astype(jnp.float32)).astype(jnp.bfloat16)


def order4(parts, place):
    low, high = (place & 1) == 1, (place & 2) == 2
    a, b, c, d = parts
    a, b, c, d = (jnp.where(low, b, a), jnp.where(low, a, b), jnp.where(low, d, c), jnp.where(low, c, d))
    return jnp.where(high, c, a), jnp.where(high, d, b), jnp.where(high, a, c), jnp.where(high, b, d)


def all_sum(values, bits):
    for axis, group in bits:
        got = [swap(values, axis, bit) for bit in group]
        values = values + got[0] if len(got) == 1 else (values + got[0]) + (got[1] + got[2])
    return values


SAMP_BITS = (("samp", (1,)), ("samp", (8,)), ("samp", (2, 4, 6)))


def scatter_chips(kept, place):
    width = kept.shape[1] // 4
    got = [
        swap(lax.dynamic_slice_in_dim(kept, (place ^ k) * width, width, 1), "samp", 2 * k) for k in (1, 2, 3)
    ]
    mine = lax.dynamic_slice_in_dim(kept, place * width, width, 1)
    mine = (mine + got[0]) + (got[1] + got[2])
    return mine + swap(mine, "samp", 8)


def gather_chips(piece, place):
    parts = [piece] + [swap(piece, "samp", 2 * k) for k in (1, 2, 3)]
    return jnp.concatenate(order4(parts, place), axis=1)


def prepare_kernel(left_ref, geno_ref, dose_ref, sums_ref, squares_ref):
    @pl.when(pl.program_id(0) == 0)
    def _():
        sums_ref[...] = jnp.zeros_like(sums_ref)
        squares_ref[...] = jnp.zeros_like(squares_ref)

    values = geno_ref[...].astype(jnp.float32)
    dose = values.astype(jnp.bfloat16)
    dose_ref[...] = dose
    sums_ref[...] += matmul(left_ref[...], dose, NN)
    squares_ref[...] += jnp.sum((values * values).reshape(-1, 8, values.shape[1]), axis=0)


def prepare(left, genotypes, tile=256):
    people, width = genotypes.shape
    return pl.pallas_call(
        prepare_kernel,
        grid=(people // tile,),
        in_specs=[pl.BlockSpec((16, tile), lambda i: (0, i)), pl.BlockSpec((tile, width), lambda i: (i, 0))],
        out_specs=[
            pl.BlockSpec((tile, width), lambda i: (i, 0)),
            pl.BlockSpec((16, width), lambda i: (0, 0)),
            pl.BlockSpec((8, width), lambda i: (0, 0)),
        ],
        out_shape=[
            jax.ShapeDtypeStruct((people, width), jnp.bfloat16),
            jax.ShapeDtypeStruct((16, width), jnp.float32),
            jax.ShapeDtypeStruct((8, width), jnp.float32),
        ],
        compiler_params=pltpu.CompilerParams(vmem_limit_bytes=VMEM),
    )(left, genotypes)


def base_rows(rows):
    row = lax.broadcasted_iota(jnp.int32, (rows, 1), 0)
    cutoff = step_size * (lambda_base * jnp.exp((row // FOLDS).astype(jnp.float32) * math.log(lambda_ratio)))
    return row, row % FOLDS, cutoff


def spread(table, fold_of):
    out = jnp.broadcast_to(table[FOLDS - 1 : FOLDS], (fold_of.shape[0], table.shape[1]))
    for fold in range(FOLDS - 1):
        out = jnp.where(fold_of == fold, table[fold : fold + 1], out)
    return out


def next_coeff(coeff, product, target, shrink, cutoff):
    gradient = (1.0 - shrink) * product + shrink * coeff - target
    return soft_threshold(coeff - step_size * gradient, cutoff)


def first_kernel(table_ref, dose_ref, out_ref, both_ref, offset_ref, total_ref):
    @pl.when(pl.program_id(0) == 0)
    def _():
        table = table_ref[...]
        row, fold_of, cutoff = base_rows(ROWS0)
        coeff = soft_threshold(step_size * spread(table[:FOLDS], fold_of), cutoff)
        scaled = jnp.where(row < BASE, coeff * table[7:8], 0.0)
        high, low = split2(scaled)
        both_ref[...] = jnp.zeros_like(both_ref)
        both_ref[0:ROWS0] = high
        both_ref[128 : 128 + ROWS0] = low
        mean_high, mean_rest = split2(table[5:6])
        rest = table[5:6] - mean_high.astype(jnp.float32)
        mean_mid, mean_low = split2(rest)
        line = lax.broadcasted_iota(jnp.int32, (16, 1), 0)
        means = jnp.where(
            line == 0,
            mean_high.astype(jnp.float32),
            jnp.where(
                line == 1,
                mean_mid.astype(jnp.float32),
                jnp.where(line == 2, mean_low.astype(jnp.float32), 0.0),
            ),
        ).astype(jnp.bfloat16)
        offset = jnp.sum(matmul(means, both_ref[...], NT), axis=0, keepdims=True)
        offset_ref[...] = jnp.broadcast_to(offset[:, :128] + offset[:, 128:], offset_ref.shape)
        total_ref[...] = jnp.zeros_like(total_ref)

    dose = dose_ref[...]
    scores = matmul(dose, both_ref[...], NT)
    scores = scores[:, :128] + scores[:, 128:] - offset_ref[0:1]
    pair = jnp.concatenate(split2(scores), axis=1)
    total_ref[...] += matmul(pair, dose, TN)

    @pl.when(pl.program_id(0) == pl.num_programs(0) - 1)
    def _():
        out_ref[...] = total_ref[0:ROWS0] + total_ref[128 : 128 + ROWS0]


def first_product(table, dose, tile=512):
    people, width = dose.shape
    return pl.pallas_call(
        first_kernel,
        grid=(people // tile,),
        in_specs=[pl.BlockSpec((8, width), lambda i: (0, 0)), pl.BlockSpec((tile, width), lambda i: (i, 0))],
        out_specs=pl.BlockSpec((ROWS0, width), lambda i: (0, 0)),
        out_shape=jax.ShapeDtypeStruct((ROWS0, width), jnp.float32),
        scratch_shapes=[
            pltpu.VMEM((256, width), jnp.bfloat16),
            pltpu.VMEM((8, 128), jnp.float32),
            pltpu.VMEM((256, width), jnp.float32),
        ],
        compiler_params=pltpu.CompilerParams(vmem_limit_bytes=VMEM),
    )(table, dose)


def second_kernel(half_ref, table_ref, product_ref, dose_ref, out_ref, coeff_ref, both_ref, offset_ref):
    rows = 2 * ROWS1

    @pl.when(pl.program_id(0) == 0)
    def _():
        table = table_ref[...]
        row, fold_of, cutoff = base_rows(ROWS1)
        target = spread(table[:FOLDS], fold_of)
        coeff = soft_threshold(step_size * target, cutoff)
        product = product_ref[0:ROWS1] * (table[7:8] / PEOPLE)
        for group in range(2):
            shrink = shrink_unit * (2 * half_ref[0] + group + 1).astype(jnp.float32)
            new = next_coeff(coeff, product, target, shrink, cutoff)
            coeff_ref[group * ROWS1 : (group + 1) * ROWS1] = jnp.where(row < BASE, new, 0.0)
        scaled = coeff_ref[...] * table[7:8]
        offset_ref[...] = jnp.sum(scaled * table[5:6], axis=1, keepdims=True)
        high, low = split2(scaled)
        both_ref[0:rows] = high
        both_ref[rows:] = low
        out_ref[...] = jnp.zeros_like(out_ref)

    dose = dose_ref[...]
    scores = matmul(both_ref[...], dose, NT)
    scores = scores[:rows] + scores[rows:] - offset_ref[...]
    pair = jnp.concatenate(split2(scores), axis=0)
    sums = matmul(pair, dose, NN)
    out_ref[...] += sums[:rows] + sums[rows:]


def second_product(half, table, product, dose, tile=512):
    people, width = dose.shape
    rows = 2 * ROWS1
    return pl.pallas_call(
        second_kernel,
        grid=(people // tile,),
        in_specs=[
            pl.BlockSpec(memory_space=pltpu.SMEM),
            pl.BlockSpec((8, width), lambda i: (0, 0)),
            pl.BlockSpec((ROWS0, width), lambda i: (0, 0)),
            pl.BlockSpec((tile, width), lambda i: (i, 0)),
        ],
        out_specs=pl.BlockSpec((rows, width), lambda i: (0, 0)),
        out_shape=jax.ShapeDtypeStruct((rows, width), jnp.float32),
        scratch_shapes=[
            pltpu.VMEM((rows, width), jnp.float32),
            pltpu.VMEM((2 * rows, width), jnp.bfloat16),
            pltpu.VMEM((rows, 1), jnp.float32),
        ],
        compiler_params=pltpu.CompilerParams(vmem_limit_bytes=VMEM),
        cost_estimate=pl.CostEstimate(
            flops=8 * people * width * rows, bytes_accessed=2 * people * width, transcendentals=0
        ),
    )(half, table, product, dose)


def predict_kernel(
    core_ref, own_ref, other_ref, table_ref, pheno_ref, fold_ref, dose_ref,
    coeff_out, number_out, score_out, coeff_ref, wide_ref, weight_ref, offset_ref,
):
    half, width = own_ref.shape

    @pl.when(pl.program_id(0) == 0)
    def _():
        def place(first_ref, second_ref):
            for lane in range(width // 128):
                lanes = slice(lane * 128, (lane + 1) * 128)
                coeff_ref[lane, 0:half] = first_ref[:, lanes]
                coeff_ref[lane, half:] = second_ref[:, lanes]
            for group in range(SHRINKS):
                ref = first_ref if group < 2 else second_ref
                start = group % 2 * ROWS1
                coeff_out[group * BASE : (group + 1) * BASE] = ref[start : start + BASE]

        @pl.when(core_ref[0] == 0)
        def _():
            place(own_ref, other_ref)

        @pl.when(core_ref[0] != 0)
        def _():
            place(other_ref, own_ref)

        for lane in range(width // 128):
            lanes = slice(lane * 128, (lane + 1) * 128)
            for fold in range(FOLDS):
                for group in range(SHRINKS):
                    first = fold * LEVELS + group * LAMBDAS
                    rows = pl.ds(group * ROWS1 + fold, LAMBDAS, FOLDS)
                    wide_ref[first : first + LAMBDAS, lanes] = coeff_ref[lane, rows]
        table = table_ref[...]
        for fold in range(FOLDS):
            span = slice(fold * LEVELS, (fold + 1) * LEVELS)
            weighted = (wide_ref[span] / table[6:7]).astype(jnp.bfloat16)
            weight_ref[span] = weighted
            wide = weighted.astype(jnp.float32)
            offset_ref[span] = jnp.sum(wide * table[5:6], axis=1, keepdims=True)
            number_out[span] = jnp.sum(wide * pheno_ref[fold : fold + 1], axis=1, keepdims=True)

    scores = matmul(weight_ref[...], dose_ref[...], NT) - offset_ref[...]
    folds = fold_ref[...]
    out = scores[0:LEVELS]
    for fold in range(1, FOLDS):
        out = jnp.where(folds == fold, scores[fold * LEVELS : (fold + 1) * LEVELS], out)
    score_out[0] = out


def predict(core, own, other, table, pheno, fold_ids, dose, parts):
    people, width = dose.shape
    half = own.shape[0]
    tile = people // parts
    whole = lambda rows: pl.BlockSpec((rows, width), lambda i: (0, 0))
    return pl.pallas_call(
        predict_kernel,
        grid=(parts,),
        in_specs=[
            pl.BlockSpec(memory_space=pltpu.SMEM),
            whole(half),
            whole(half),
            whole(8),
            whole(FOLDS),
            pl.BlockSpec((1, tile), lambda i: (0, i)),
            pl.BlockSpec((tile, width), lambda i: (i, 0)),
        ],
        out_specs=[
            whole(GRID),
            pl.BlockSpec((GRID, 1), lambda i: (0, 0)),
            pl.BlockSpec((1, LEVELS, tile), lambda i: (i, 0, 0)),
        ],
        out_shape=[
            jax.ShapeDtypeStruct((GRID, width), jnp.float32),
            jax.ShapeDtypeStruct((GRID, 1), jnp.float32),
            jax.ShapeDtypeStruct((parts, LEVELS, tile), jnp.float32),
        ],
        scratch_shapes=[
            pltpu.VMEM((width // 128, 2 * half, 128), jnp.float32),
            pltpu.VMEM((GRID, width), jnp.float32),
            pltpu.VMEM((GRID, width), jnp.bfloat16),
            pltpu.VMEM((GRID, 1), jnp.float32),
        ],
        compiler_params=pltpu.CompilerParams(vmem_limit_bytes=VMEM),
    )(core, own, other, table, pheno, fold_ids.reshape(1, people), dose)


def local(genotypes, phenotype, fold_ids):
    num_rows, block_width = genotypes.shape
    samp, blk = lax.axis_index("samp"), lax.axis_index("blk")
    core, place = samp & 1, (samp >> 1) & 3

    onehot = fold_ids[None, :] == jnp.arange(FOLDS)[:, None]
    pheno_split = jnp.where(onehot, phenotype[None, :], 0.0)
    high = rounded(pheno_split)
    mid = rounded(pheno_split - high)
    low = pheno_split - high - mid
    ones = jnp.ones((1, num_rows), jnp.float32)
    left = jnp.concatenate([high, mid, low, ones], axis=0).astype(jnp.bfloat16)
    dose, parts, squares = prepare(left, genotypes)
    counts = jnp.sum(onehot.astype(jnp.float32), axis=1)
    fold_sum = jnp.sum(pheno_split, axis=1)
    extra = jnp.concatenate([counts, fold_sum, jnp.zeros((block_width - 2 * FOLDS,), jnp.float32)])
    stats = jnp.concatenate(
        [
            parts[:5] + parts[5:10] + parts[10:15],
            parts[15:16],
            jnp.sum(squares, axis=0, keepdims=True),
            extra[None],
        ],
        axis=0,
    )
    stats = all_sum(stats, SAMP_BITS)
    geno_pheno = stats[:FOLDS]
    fold_count = stats[7, :FOLDS][:, None]
    fold_pheno_sum = stats[7, FOLDS : 2 * FOLDS][:, None]
    snp_mean = stats[5:6] / PEOPLE
    scales = jnp.sqrt(stats[6:7] / PEOPLE - snp_mean * snp_mean + epsilon)
    train_geno = jnp.sum(geno_pheno, axis=0, keepdims=True) - geno_pheno
    train_pheno = jnp.sum(fold_pheno_sum) - fold_pheno_sum
    zscore = (train_geno - train_pheno * snp_mean) / (scales * jnp.sqrt(PEOPLE - fold_count))
    table = jnp.concatenate([zscore, snp_mean, scales, 1.0 / scales], axis=0)

    part = first_product(table, dose)
    rows = ROWS0 // 2
    kept = lax.dynamic_slice_in_dim(part, core * rows, rows, 0)
    sent = lax.dynamic_slice_in_dim(part, (1 - core) * rows, rows, 0)
    piece = scatter_chips(kept + swap(sent, "samp", 1), place)
    own = gather_chips(piece, place)
    other = swap(own, "samp", 1)
    first = core == 0
    product = jnp.concatenate([jnp.where(first, own, other), jnp.where(first, other, own)], axis=0)

    sent = second_product((1 - core)[None], table, product, dose)
    sent = swap(sent, "samp", 1)
    kept = second_product(core[None], table, product, dose)
    piece = scatter_chips(kept + sent, place)
    width = block_width // 4
    here = lambda a: lax.dynamic_slice_in_dim(a, place * width, width, 1)
    row, fold_of, cutoff = base_rows(ROWS1)
    table_here = here(table)
    target = spread(table_here[:FOLDS], fold_of)
    coeff = soft_threshold(step_size * target, cutoff)
    scale_here = table_here[7:8] / PEOPLE
    old = here(product[:ROWS1]) * scale_here
    final = []
    for group in range(2):
        shrink = shrink_unit * (2 * core + group + 1).astype(jnp.float32)
        new = next_coeff(coeff, old, target, shrink, cutoff)
        latest = piece[group * ROWS1 : (group + 1) * ROWS1] * scale_here
        final.append(next_coeff(new, latest, target, shrink, cutoff))
    own = gather_chips(jnp.concatenate(final, axis=0), place)
    other = swap(own, "samp", 1)

    centred_pheno = geno_pheno - snp_mean * fold_pheno_sum
    blocks = lax.axis_size("blk")
    coeff_all, numerator, scores = predict(core[None], own, other, table, centred_pheno, fold_ids, dose, blocks)
    scores = jnp.sum(lax.all_to_all(scores, "blk", 0, 0, tiled=True), axis=0)
    people = num_rows // blocks
    folds_here = lax.dynamic_slice_in_dim(fold_ids, blk * people, people, 0)
    square = scores * scores
    denominator = jnp.stack(
        [jnp.sum(jnp.where((folds_here == fold)[None, :], square, 0.0), axis=1) for fold in range(FOLDS)]
    )
    sums = jnp.stack([numerator.reshape(FOLDS, LEVELS) / lax.axis_size("samp"), denominator])
    sums = all_sum(sums, SAMP_BITS + (("blk", (4,)), ("blk", (1, 2, 3))))
    sums = sums * jnp.array([1.0 / math.sqrt(SNPS), 1.0 / SNPS], jnp.float32)[:, None, None] / fold_count[None]
    fold_scores = sums.transpose(0, 2, 1).reshape(2, GRID)
    return (coeff_all.T, fold_scores)


def solution(mesh):
    return jax.shard_map(
        local,
        mesh=mesh,
        in_specs=(P("samp", "blk"), P("samp"), P("samp")),
        out_specs=(P("blk", None), P()),
        check_vma=False,
    )
```

```python
import functools
import math

import jax
import jax.numpy as jnp
from jax import lax
from jax.experimental import pallas as pl
from jax.experimental.pallas import tpu as pltpu
from jax.sharding import PartitionSpec as P

FOLDS = 5
LAMBDAS = 20
GRID = 400
BASE = FOLDS * LAMBDAS
SHRINKS = GRID // BASE
LEVELS = GRID // FOLDS
ROWS0 = 112
ROWS1 = 104
PEOPLE = 32768
SNPS = 12288
VMEM = 36 * 1024 * 1024
TILE = 512

step_size = 0.6
epsilon = 1e-05
lambda_base = 0.1
lambda_ratio = 1.2
shrink_unit = 0.2

NT = (((1,), (1,)), ((), ()))
NN = (((1,), (0,)), ((), ()))
TN = (((0,), (0,)), ((), ()))


def matmul(left, right, dims):
    return lax.dot_general(left, right, dims, preferred_element_type=jnp.float32)


def soft_threshold(values, cutoff):
    return values - jnp.clip(values, -cutoff, cutoff)


def swap(values, axis, bit):
    size = lax.axis_size(axis)
    return lax.ppermute(values, axis, [(i, i ^ bit) for i in range(size)])


def split2(values):
    high = values.astype(jnp.bfloat16)
    return high, (values - high.astype(jnp.float32)).astype(jnp.bfloat16)


def order4(parts, place):
    low, high = (place & 1) == 1, (place & 2) == 2
    a, b, c, d = parts
    a, b, c, d = (jnp.where(low, b, a), jnp.where(low, a, b), jnp.where(low, d, c), jnp.where(low, c, d))
    return jnp.where(high, c, a), jnp.where(high, d, b), jnp.where(high, a, c), jnp.where(high, b, d)


def all_sum(values, bits):
    for axis, group in bits:
        got = [swap(values, axis, bit) for bit in group]
        values = values + got[0] if len(got) == 1 else (values + got[0]) + (got[1] + got[2])
    return values


BOTH = ("samp", "blk")
SAMP_BITS = (("samp", (1,)), ("samp", (8,)), ("samp", (2, 4, 6)))
ALL_BITS = (("samp", (1,)), ("samp", (2, 4, 6)), ("blk", (1, 2, 3)), (BOTH, (4, 64, 68)))


def scatter_chips(kept, place):
    width = kept.shape[1] // 4
    got = [
        swap(lax.dynamic_slice_in_dim(kept, (place ^ k) * width, width, 1), "samp", 2 * k) for k in (1, 2, 3)
    ]
    mine = lax.dynamic_slice_in_dim(kept, place * width, width, 1)
    mine = (mine + got[0]) + (got[1] + got[2])
    return mine + swap(mine, "samp", 8)


def gather_chips(piece, place):
    parts = [piece] + [swap(piece, "samp", 2 * k) for k in (1, 2, 3)]
    return jnp.concatenate(order4(parts, place), axis=1)


def whole(count):
    return [pl.BlockSpec(memory_space=pltpu.VMEM)] * count


def params():
    return pltpu.CompilerParams(vmem_limit_bytes=VMEM)


def parts3(values):
    high, rest = split2(values)
    rest = values - high.astype(jnp.float32)
    mid, low = split2(rest)
    return [part.astype(jnp.float32) for part in (high, mid, low)]


def prepare_kernel(pheno_ref, fold_ref, geno_ref, dose_ref, stats_ref, buffer_ref, left_ref, sums_ref, sems):
    people, width = dose_ref.shape
    parts = sems.shape[0]
    tile = people // parts
    copies = [
        pltpu.make_async_copy(
            geno_ref.at[pl.ds(part * tile, tile)], buffer_ref.at[pl.ds(part * tile, tile)], sems.at[part]
        )
        for part in range(parts)
    ]
    for copy in copies:
        copy.start()
    line = lax.broadcasted_iota(jnp.int32, (8, people), 0)
    chosen = line == fold_ref[...]
    split = jnp.where(chosen, pheno_ref[...], 0.0)
    high, mid, low = parts3(split)
    high = jnp.where(line == FOLDS, 1.0, high)
    left_ref[...] = jnp.concatenate([high, mid, low, jnp.zeros_like(low)], axis=0).astype(jnp.bfloat16)
    counts = jnp.sum(chosen.astype(jnp.float32), axis=1, keepdims=True)
    sums = jnp.sum(split, axis=1, keepdims=True)
    lane = lax.broadcasted_iota(jnp.int32, (1, width), 1)
    extra = jnp.zeros((1, width), jnp.float32)
    for fold in range(FOLDS):
        extra = jnp.where(lane == fold, counts[fold : fold + 1], extra)
        extra = jnp.where(lane == FOLDS + fold, sums[fold : fold + 1], extra)
    squares = jnp.zeros((8, width), jnp.float32)
    for part in range(parts):
        copies[part].wait()
        span = slice(part * tile, (part + 1) * tile)
        values = buffer_ref[span].astype(jnp.float32)
        dose = values.astype(jnp.bfloat16)
        dose_ref[span] = dose
        product = matmul(left_ref[:, span], dose, NN)
        sums_ref[...] = product if part == 0 else sums_ref[...] + product
        squares += jnp.sum((values * values).reshape(-1, 8, width), axis=0)
    stats_ref[0:8] = sums_ref[0:8] + sums_ref[8:16] + sums_ref[16:24]
    stats_ref[6:7] = jnp.sum(squares, axis=0, keepdims=True)
    stats_ref[7:8] = extra


def prepare(genotypes, phenotype, fold_ids, parts=8):
    people, width = genotypes.shape
    return pl.pallas_call(
        prepare_kernel,
        in_specs=whole(2) + [pl.BlockSpec(memory_space=pl.ANY)],
        out_specs=whole(2),
        out_shape=[
            jax.ShapeDtypeStruct((people, width), jnp.bfloat16),
            jax.ShapeDtypeStruct((8, width), jnp.float32),
        ],
        scratch_shapes=[
            pltpu.VMEM((people, width), jnp.int32),
            pltpu.VMEM((32, people), jnp.bfloat16),
            pltpu.VMEM((32, width), jnp.float32),
            pltpu.SemaphoreType.DMA((parts,)),
        ],
        compiler_params=params(),
    )(phenotype.reshape(1, people), fold_ids.reshape(1, people), genotypes)


def base_rows(rows):
    row = lax.broadcasted_iota(jnp.int32, (rows, 1), 0)
    cutoff = step_size * (lambda_base * jnp.exp((row // FOLDS).astype(jnp.float32) * math.log(lambda_ratio)))
    return row, row % FOLDS, cutoff


def spread(table, fold_of):
    out = jnp.broadcast_to(table[FOLDS - 1 : FOLDS], (fold_of.shape[0], table.shape[1]))
    for fold in range(FOLDS - 1):
        out = jnp.where(fold_of == fold, table[fold : fold + 1], out)
    return out


def next_coeff(coeff, product, target, shrink, cutoff):
    gradient = (1.0 - shrink) * product + shrink * coeff - target
    return soft_threshold(coeff - step_size * gradient, cutoff)


def first_kernel(core_ref, stats_ref, dose_ref, kept_ref, sent_ref, table_ref, both_ref, total_ref):
    stats = stats_ref[...]
    mean = stats[5:6] / PEOPLE
    scales = jnp.sqrt(stats[6:7] / PEOPLE - mean * mean + epsilon)
    inverse = 1.0 / scales
    lane = lax.broadcasted_iota(jnp.int32, (1, stats.shape[1]), 1)
    pick = lambda place: jnp.sum(jnp.where(lane == place, stats[7:8], 0.0), axis=1, keepdims=True)
    counts = [pick(fold) for fold in range(FOLDS)]
    sums = [pick(FOLDS + fold) for fold in range(FOLDS)]
    every = sums[0] + sums[1] + sums[2] + sums[3] + sums[4]
    geno_pheno = jnp.sum(stats[0:FOLDS], axis=0, keepdims=True)
    row, fold_of, cutoff = base_rows(ROWS0)
    target = jnp.zeros((ROWS0, stats.shape[1]), jnp.float32)
    for fold in range(FOLDS):
        train = geno_pheno - stats[fold : fold + 1]
        zscore = (train - (every - sums[fold]) * mean) / (scales * jnp.sqrt(PEOPLE - counts[fold]))
        table_ref[fold : fold + 1] = zscore
        table_ref[8 + fold : 9 + fold] = stats[fold : fold + 1] - mean * sums[fold]
        target = jnp.where(fold_of == fold, zscore, target)
    table_ref[5:6] = mean
    table_ref[6:7] = scales
    table_ref[7:8] = inverse
    table_ref[13:16] = jnp.zeros((3, stats.shape[1]), jnp.float32)
    coeff = soft_threshold(step_size * target, cutoff)
    scaled = jnp.where(row < BASE, coeff * inverse, 0.0)
    high, low = split2(scaled)
    both_ref[...] = jnp.zeros_like(both_ref)
    both_ref[0:ROWS0] = high
    both_ref[128 : 128 + ROWS0] = low
    line = lax.broadcasted_iota(jnp.int32, (16, 1), 0)
    mean_high, mean_mid, mean_low = parts3(mean)
    means = jnp.where(line == 0, mean_high, jnp.where(line == 1, mean_mid, jnp.where(line == 2, mean_low, 0.0)))
    offset = jnp.sum(matmul(means.astype(jnp.bfloat16), both_ref[...], NT), axis=0, keepdims=True)
    offset = offset[:, :128] + offset[:, 128:]
    total_ref[...] = jnp.zeros_like(total_ref)

    def body(step, carry):
        dose = dose_ref[pl.ds(pl.multiple_of(step * TILE, TILE), TILE)]
        scores = matmul(dose, both_ref[...], NT)
        scores = scores[:, :128] + scores[:, 128:] - carry
        pair = jnp.concatenate(split2(scores), axis=1)
        total_ref[...] += matmul(pair, dose, TN)
        return carry

    lax.fori_loop(0, dose_ref.shape[0] // TILE, body, offset)
    half = ROWS0 // 2
    first = total_ref[0:half] + total_ref[128 : 128 + half]
    second = total_ref[half:ROWS0] + total_ref[128 + half : 128 + ROWS0]
    is_first = core_ref[0] == 0
    kept_ref[...] = jnp.where(is_first, first, second)
    sent_ref[...] = jnp.where(is_first, second, first)


def first_product(core, stats, dose):
    width = dose.shape[1]
    half = jax.ShapeDtypeStruct((ROWS0 // 2, width), jnp.float32)
    return pl.pallas_call(
        first_kernel,
        in_specs=[pl.BlockSpec(memory_space=pltpu.SMEM)] + whole(2),
        out_specs=whole(3),
        out_shape=[half, half, jax.ShapeDtypeStruct((16, width), jnp.float32)],
        scratch_shapes=[pltpu.VMEM((256, width), jnp.bfloat16), pltpu.VMEM((256, width), jnp.float32)],
        compiler_params=params(),
    )(core, stats, dose)


def second_kernel(
    core_ref, table_ref, own_ref, other_ref, dose_ref, out_ref, product_ref, coeff_ref, both_ref, *, mine
):
    rows = 2 * ROWS1
    half = ROWS0 // 2
    table = table_ref[...]
    row, fold_of, cutoff = base_rows(ROWS1)
    target = spread(table[:FOLDS], fold_of)
    coeff = soft_threshold(step_size * target, cutoff)
    is_first = core_ref[0] == 0
    product_ref[0:half] = jnp.where(is_first, own_ref[...], other_ref[...])
    product_ref[half:] = jnp.where(is_first, other_ref[...], own_ref[...])
    product = product_ref[0:ROWS1] * (table[7:8] / PEOPLE)
    side = core_ref[0] if mine else 1 - core_ref[0]
    for group in range(2):
        shrink = shrink_unit * (2 * side + group + 1).astype(jnp.float32)
        new = next_coeff(coeff, product, target, shrink, cutoff)
        coeff_ref[group * ROWS1 : (group + 1) * ROWS1] = jnp.where(row < BASE, new, 0.0)
    scaled = coeff_ref[...] * table[7:8]
    offset = jnp.sum(scaled * table[5:6], axis=1, keepdims=True)
    high, low = split2(scaled)
    both_ref[0:rows] = high
    both_ref[rows:] = low
    out_ref[...] = jnp.zeros_like(out_ref)

    def body(step, carry):
        dose = dose_ref[pl.ds(pl.multiple_of(step * TILE, TILE), TILE)]
        scores = matmul(both_ref[...], dose, NT)
        scores = scores[:rows] + scores[rows:] - carry
        pair = jnp.concatenate(split2(scores), axis=0)
        sums = matmul(pair, dose, NN)
        out_ref[...] += sums[:rows] + sums[rows:]
        return carry

    lax.fori_loop(0, dose_ref.shape[0] // TILE, body, offset)


def second_product(core, table, own, other, dose, mine):
    people, width = dose.shape
    rows = 2 * ROWS1
    return pl.pallas_call(
        functools.partial(second_kernel, mine=mine),
        in_specs=[pl.BlockSpec(memory_space=pltpu.SMEM)] + whole(4),
        out_specs=pl.BlockSpec(memory_space=pltpu.VMEM),
        out_shape=jax.ShapeDtypeStruct((rows, width), jnp.float32),
        scratch_shapes=[
            pltpu.VMEM((ROWS0, width), jnp.float32),
            pltpu.VMEM((rows, width), jnp.float32),
            pltpu.VMEM((2 * rows, width), jnp.bfloat16),
        ],
        compiler_params=params(),
        cost_estimate=pl.CostEstimate(
            flops=8 * people * width * rows, bytes_accessed=2 * people * width, transcendentals=0
        ),
    )(core, table, own, other, dose)


def predict_kernel(
    core_ref, own_ref, other_ref, table_ref, fold_ref, dose_ref,
    coeff_out, number_out, score_out, coeff_ref, wide_ref, weight_ref, offset_ref,
):
    half, width = own_ref.shape

    def place(first_ref, second_ref):
        for lane in range(width // 128):
            lanes = slice(lane * 128, (lane + 1) * 128)
            coeff_ref[lane, 0:half] = first_ref[:, lanes]
            coeff_ref[lane, half:] = second_ref[:, lanes]
        for group in range(SHRINKS):
            ref = first_ref if group < 2 else second_ref
            start = group % 2 * ROWS1
            coeff_out[group * BASE : (group + 1) * BASE] = ref[start : start + BASE]

    @pl.when(core_ref[0] == 0)
    def _():
        place(own_ref, other_ref)

    @pl.when(core_ref[0] != 0)
    def _():
        place(other_ref, own_ref)

    for lane in range(width // 128):
        lanes = slice(lane * 128, (lane + 1) * 128)
        for fold in range(FOLDS):
            for group in range(SHRINKS):
                first = fold * LEVELS + group * LAMBDAS
                rows = pl.ds(group * ROWS1 + fold, LAMBDAS, FOLDS)
                wide_ref[first : first + LAMBDAS, lanes] = coeff_ref[lane, rows]
    table = table_ref[...]
    for fold in range(FOLDS):
        span = slice(fold * LEVELS, (fold + 1) * LEVELS)
        weighted = (wide_ref[span] / table[6:7]).astype(jnp.bfloat16)
        weight_ref[span] = weighted
        wide = weighted.astype(jnp.float32)
        offset_ref[span] = jnp.sum(wide * table[5:6], axis=1, keepdims=True)
        number_out[span] = jnp.sum(wide * table[8 + fold : 9 + fold], axis=1, keepdims=True)

    parts, _, tile = score_out.shape

    def body(part, carry):
        start = pl.multiple_of(part * tile, tile)
        scores = matmul(weight_ref[...], dose_ref[pl.ds(start, tile)], NT) - offset_ref[...]
        folds = fold_ref[:, pl.ds(start, tile)]
        out = scores[0:LEVELS]
        for fold in range(1, FOLDS):
            out = jnp.where(folds == fold, scores[fold * LEVELS : (fold + 1) * LEVELS], out)
        score_out[part] = out
        return carry

    lax.fori_loop(0, parts, body, 0)


def predict(core, own, other, table, fold_ids, dose, parts):
    people, width = dose.shape
    half = own.shape[0]
    return pl.pallas_call(
        predict_kernel,
        in_specs=[pl.BlockSpec(memory_space=pltpu.SMEM)] + whole(5),
        out_specs=whole(3),
        out_shape=[
            jax.ShapeDtypeStruct((GRID, width), jnp.float32),
            jax.ShapeDtypeStruct((GRID, 1), jnp.float32),
            jax.ShapeDtypeStruct((parts, LEVELS, people // parts), jnp.float32),
        ],
        scratch_shapes=[
            pltpu.VMEM((width // 128, 2 * half, 128), jnp.float32),
            pltpu.VMEM((GRID, width), jnp.float32),
            pltpu.VMEM((GRID, width), jnp.bfloat16),
            pltpu.VMEM((GRID, 1), jnp.float32),
        ],
        compiler_params=params(),
    )(core, own, other, table, fold_ids.reshape(1, people), dose)


def local(genotypes, phenotype, fold_ids):
    num_rows, block_width = genotypes.shape
    samp, blk = lax.axis_index("samp"), lax.axis_index("blk")
    core, place = samp & 1, (samp >> 1) & 3

    dose, stats = prepare(genotypes, phenotype, fold_ids)
    stats = all_sum(stats, SAMP_BITS)
    fold_count = stats[7, :FOLDS][:, None]

    kept, sent, table = first_product(core[None], stats, dose)
    piece = scatter_chips(kept + swap(sent, "samp", 1), place)
    own_product = gather_chips(piece, place)
    other_product = swap(own_product, "samp", 1)

    sent = second_product(core[None], table, own_product, other_product, dose, False)
    sent = swap(sent, "samp", 1)
    kept = second_product(core[None], table, own_product, other_product, dose, True)
    piece = scatter_chips(kept + sent, place)
    width = block_width // 4
    here = lambda a: lax.dynamic_slice_in_dim(a, place * width, width, 1)
    row, fold_of, cutoff = base_rows(ROWS1)
    table_here = here(table)
    target = spread(table_here[:FOLDS], fold_of)
    coeff = soft_threshold(step_size * target, cutoff)
    scale_here = table_here[7:8] / PEOPLE
    first = core == 0
    own, other = here(own_product), here(other_product)
    old = jnp.concatenate([jnp.where(first, own, other), jnp.where(first, other, own)], axis=0)
    old = old[:ROWS1] * scale_here
    final = []
    for group in range(2):
        shrink = shrink_unit * (2 * core + group + 1).astype(jnp.float32)
        new = next_coeff(coeff, old, target, shrink, cutoff)
        latest = piece[group * ROWS1 : (group + 1) * ROWS1] * scale_here
        final.append(next_coeff(new, latest, target, shrink, cutoff))
    own = gather_chips(jnp.concatenate(final, axis=0), place)
    other = swap(own, "samp", 1)

    blocks = lax.axis_size("blk")
    coeff_all, numerator, scores = predict(core[None], own, other, table, fold_ids, dose, blocks)
    scores = jnp.sum(lax.all_to_all(scores, "blk", 0, 0, tiled=True), axis=0)
    people = num_rows // blocks
    folds_here = lax.dynamic_slice_in_dim(fold_ids, blk * people, people, 0)
    square = scores * scores
    denominator = jnp.stack(
        [jnp.sum(jnp.where((folds_here == fold)[None, :], square, 0.0), axis=1) for fold in range(FOLDS)]
    )
    sums = jnp.stack([numerator.reshape(FOLDS, LEVELS) / lax.axis_size("samp"), denominator])
    sums = all_sum(sums, ALL_BITS)
    sums = sums * jnp.array([1.0 / math.sqrt(SNPS), 1.0 / SNPS], jnp.float32)[:, None, None] / fold_count[None]
    fold_scores = sums.transpose(0, 2, 1).reshape(2, GRID)
    return (coeff_all.T, fold_scores)


def solution(mesh):
    return jax.shard_map(
        local,
        mesh=mesh,
        in_specs=(P("samp", "blk"), P("samp"), P("samp")),
        out_specs=(P("blk", None), P()),
        check_vma=False,
    )
```

```python
import functools
import math

import jax
import jax.numpy as jnp
from jax import lax
from jax.experimental import pallas as pl
from jax.experimental.pallas import tpu as pltpu
from jax.sharding import PartitionSpec as P

FOLDS = 5
LAMBDAS = 20
GRID = 400
BASE = FOLDS * LAMBDAS
SHRINKS = GRID // BASE
LEVELS = GRID // FOLDS
ROWS0 = 112
ROWS1 = 104
PEOPLE = 32768
SNPS = 12288
VMEM = 36 * 1024 * 1024
TILE = 512

step_size = 0.6
epsilon = 1e-05
lambda_base = 0.1
lambda_ratio = 1.2
shrink_unit = 0.2

NT = (((1,), (1,)), ((), ()))
NN = (((1,), (0,)), ((), ()))
TN = (((0,), (0,)), ((), ()))


def matmul(left, right, dims):
    return lax.dot_general(left, right, dims, preferred_element_type=jnp.float32)


def soft_threshold(values, cutoff):
    return values - jnp.clip(values, -cutoff, cutoff)


def swap(values, axis, bit):
    size = lax.axis_size(axis)
    return lax.ppermute(values, axis, [(i, i ^ bit) for i in range(size)])


def split2(values):
    high = values.astype(jnp.bfloat16)
    return high, (values - high.astype(jnp.float32)).astype(jnp.bfloat16)


def all_sum(values, bits):
    for axis, group in bits:
        got = [swap(values, axis, bit) for bit in group]
        values = values + got[0] if len(got) == 1 else (values + got[0]) + (got[1] + got[2])
    return values


BOTH = ("samp", "blk")
SAMP_BITS = (("samp", (1,)), ("samp", (8,)), ("samp", (2, 4, 6)))
ALL_BITS = (("samp", (1,)), ("samp", (2, 4, 6)), ("blk", (1, 2, 3)), (BOTH, (4, 64, 68)))


def here():
    samp = lax.axis_index("samp")
    return samp & 1, (samp >> 1) & 3


def split_kernel(kept_ref, got_ref, *out_refs):
    width = out_refs[0].shape[1]
    place = here()[1]
    for k, out_ref in enumerate(out_refs):
        lanes = pl.ds(pl.multiple_of((place ^ k) * width, 128), width)
        out_ref[...] = kept_ref[:, lanes] + got_ref[:, lanes]


def scatter_chips(kept, got):
    rows, width = kept.shape
    mine, *sent = pl.pallas_call(
        split_kernel,
        in_specs=whole(2),
        out_specs=whole(4),
        out_shape=[jax.ShapeDtypeStruct((rows, width // 4), jnp.float32)] * 4,
        compiler_params=params(),
    )(kept, got)
    got = [swap(part, "samp", 2 * k) for k, part in zip((1, 2, 3), sent)]
    return (mine + got[0]) + (got[1] + got[2])


def gather_chips(piece):
    own = jnp.stack([piece] + [swap(piece, "samp", 2 * k) for k in (1, 2, 3)])
    return own, swap(own, "samp", 1)


def lanes_of(place, k, width):
    return pl.ds(pl.multiple_of((place ^ k) * width, 128), width)


def whole(count):
    return [pl.BlockSpec(memory_space=pltpu.VMEM)] * count


def params():
    return pltpu.CompilerParams(vmem_limit_bytes=VMEM)


def parts3(values):
    high, rest = split2(values)
    rest = values - high.astype(jnp.float32)
    mid, low = split2(rest)
    return [part.astype(jnp.float32) for part in (high, mid, low)]


def prepare_kernel(pheno_ref, fold_ref, geno_ref, dose_ref, stats_ref, buffer_ref, left_ref, sums_ref, sems):
    people, width = dose_ref.shape
    parts = sems.shape[0]
    tile = people // parts
    copies = [
        pltpu.make_async_copy(
            geno_ref.at[pl.ds(part * tile, tile)], buffer_ref.at[pl.ds(part * tile, tile)], sems.at[part]
        )
        for part in range(parts)
    ]
    for copy in copies:
        copy.start()
    line = lax.broadcasted_iota(jnp.int32, (8, people), 0)
    chosen = line == fold_ref[...]
    split = jnp.where(chosen, pheno_ref[...], 0.0)
    high, mid, low = parts3(split)
    high = jnp.where(line == FOLDS, 1.0, high)
    left_ref[...] = jnp.concatenate([high, mid, low, jnp.zeros_like(low)], axis=0).astype(jnp.bfloat16)
    counts = jnp.sum(chosen.astype(jnp.float32), axis=1, keepdims=True)
    sums = jnp.sum(split, axis=1, keepdims=True)
    lane = lax.broadcasted_iota(jnp.int32, (1, width), 1)
    extra = jnp.zeros((1, width), jnp.float32)
    for fold in range(FOLDS):
        extra = jnp.where(lane == fold, counts[fold : fold + 1], extra)
        extra = jnp.where(lane == FOLDS + fold, sums[fold : fold + 1], extra)
    squares = jnp.zeros((8, width), jnp.float32)
    for part in range(parts):
        copies[part].wait()
        span = slice(part * tile, (part + 1) * tile)
        values = buffer_ref[span].astype(jnp.float32)
        dose = values.astype(jnp.bfloat16)
        dose_ref[span] = dose
        product = matmul(left_ref[:, span], dose, NN)
        sums_ref[...] = product if part == 0 else sums_ref[...] + product
        squares += jnp.sum((values * values).reshape(-1, 8, width), axis=0)
    stats_ref[0:8] = sums_ref[0:8] + sums_ref[8:16] + sums_ref[16:24]
    stats_ref[6:7] = jnp.sum(squares, axis=0, keepdims=True)
    stats_ref[7:8] = extra


def prepare(genotypes, phenotype, fold_ids, parts=8):
    people, width = genotypes.shape
    return pl.pallas_call(
        prepare_kernel,
        in_specs=whole(2) + [pl.BlockSpec(memory_space=pl.ANY)],
        out_specs=whole(2),
        out_shape=[
            jax.ShapeDtypeStruct((people, width), jnp.bfloat16),
            jax.ShapeDtypeStruct((8, width), jnp.float32),
        ],
        scratch_shapes=[
            pltpu.VMEM((people, width), jnp.int32),
            pltpu.VMEM((32, people), jnp.bfloat16),
            pltpu.VMEM((32, width), jnp.float32),
            pltpu.SemaphoreType.DMA((parts,)),
        ],
        compiler_params=params(),
    )(phenotype.reshape(1, people), fold_ids.reshape(1, people), genotypes)


def base_rows(rows):
    row = lax.broadcasted_iota(jnp.int32, (rows, 1), 0)
    cutoff = step_size * (lambda_base * jnp.exp((row // FOLDS).astype(jnp.float32) * math.log(lambda_ratio)))
    return row, row % FOLDS, cutoff


def spread(table, fold_of):
    out = jnp.broadcast_to(table[FOLDS - 1 : FOLDS], (fold_of.shape[0], table.shape[1]))
    for fold in range(FOLDS - 1):
        out = jnp.where(fold_of == fold, table[fold : fold + 1], out)
    return out


def next_coeff(coeff, product, target, shrink, cutoff):
    gradient = (1.0 - shrink) * product + shrink * coeff - target
    return soft_threshold(coeff - step_size * gradient, cutoff)


def first_kernel(stats_ref, dose_ref, kept_ref, sent_ref, table_ref, both_ref, total_ref):
    stats = stats_ref[...]
    mean = stats[5:6] / PEOPLE
    scales = jnp.sqrt(stats[6:7] / PEOPLE - mean * mean + epsilon)
    inverse = 1.0 / scales
    lane = lax.broadcasted_iota(jnp.int32, (1, stats.shape[1]), 1)
    pick = lambda place: jnp.sum(jnp.where(lane == place, stats[7:8], 0.0), axis=1, keepdims=True)
    counts = [pick(fold) for fold in range(FOLDS)]
    sums = [pick(FOLDS + fold) for fold in range(FOLDS)]
    every = sums[0] + sums[1] + sums[2] + sums[3] + sums[4]
    geno_pheno = jnp.sum(stats[0:FOLDS], axis=0, keepdims=True)
    row, fold_of, cutoff = base_rows(ROWS0)
    target = jnp.zeros((ROWS0, stats.shape[1]), jnp.float32)
    for fold in range(FOLDS):
        train = geno_pheno - stats[fold : fold + 1]
        zscore = (train - (every - sums[fold]) * mean) / (scales * jnp.sqrt(PEOPLE - counts[fold]))
        table_ref[fold : fold + 1] = zscore
        table_ref[8 + fold : 9 + fold] = stats[fold : fold + 1] - mean * sums[fold]
        target = jnp.where(fold_of == fold, zscore, target)
    table_ref[5:6] = mean
    table_ref[6:7] = scales
    table_ref[7:8] = inverse
    table_ref[13:16] = jnp.zeros((3, stats.shape[1]), jnp.float32)
    coeff = soft_threshold(step_size * target, cutoff)
    scaled = jnp.where(row < BASE, coeff * inverse, 0.0)
    high, low = split2(scaled)
    both_ref[...] = jnp.zeros_like(both_ref)
    both_ref[0:ROWS0] = high
    both_ref[128 : 128 + ROWS0] = low
    line = lax.broadcasted_iota(jnp.int32, (16, 1), 0)
    mean_high, mean_mid, mean_low = parts3(mean)
    means = jnp.where(line == 0, mean_high, jnp.where(line == 1, mean_mid, jnp.where(line == 2, mean_low, 0.0)))
    offset = jnp.sum(matmul(means.astype(jnp.bfloat16), both_ref[...], NT), axis=0, keepdims=True)
    offset = offset[:, :128] + offset[:, 128:]
    total_ref[...] = jnp.zeros_like(total_ref)

    def body(step, carry):
        dose = dose_ref[pl.ds(pl.multiple_of(step * TILE, TILE), TILE)]
        scores = matmul(dose, both_ref[...], NT)
        scores = scores[:, :128] + scores[:, 128:] - carry
        pair = jnp.concatenate(split2(scores), axis=1)
        total_ref[...] += matmul(pair, dose, TN)
        return carry

    lax.fori_loop(0, dose_ref.shape[0] // TILE, body, offset)
    half = ROWS0 // 2
    first = total_ref[0:half] + total_ref[128 : 128 + half]
    second = total_ref[half:ROWS0] + total_ref[128 + half : 128 + ROWS0]
    is_first = here()[0] == 0
    kept_ref[...] = jnp.where(is_first, first, second)
    sent_ref[...] = jnp.where(is_first, second, first)


def first_product(stats, dose):
    width = dose.shape[1]
    half = jax.ShapeDtypeStruct((ROWS0 // 2, width), jnp.float32)
    return pl.pallas_call(
        first_kernel,
        in_specs=whole(2),
        out_specs=whole(3),
        out_shape=[half, half, jax.ShapeDtypeStruct((16, width), jnp.float32)],
        scratch_shapes=[pltpu.VMEM((256, width), jnp.bfloat16), pltpu.VMEM((256, width), jnp.float32)],
        compiler_params=params(),
    )(stats, dose)


def second_kernel(
    table_ref, own_ref, other_ref, dose_ref, out_ref, product_ref, coeff_ref, both_ref, *, mine
):
    rows = 2 * ROWS1
    half = ROWS0 // 2
    table = table_ref[...]
    row, fold_of, cutoff = base_rows(ROWS1)
    target = spread(table[:FOLDS], fold_of)
    coeff = soft_threshold(step_size * target, cutoff)
    core, place = here()
    for k in range(4):
        lanes = lanes_of(place, k, own_ref.shape[2])
        product_ref[0:half, lanes] = jnp.where(core == 0, own_ref[k], other_ref[k])
        product_ref[half:, lanes] = jnp.where(core == 0, other_ref[k], own_ref[k])
    product = product_ref[0:ROWS1] * (table[7:8] / PEOPLE)
    side = core if mine else 1 - core
    for group in range(2):
        shrink = shrink_unit * (2 * side + group + 1).astype(jnp.float32)
        new = next_coeff(coeff, product, target, shrink, cutoff)
        coeff_ref[group * ROWS1 : (group + 1) * ROWS1] = jnp.where(row < BASE, new, 0.0)
    scaled = coeff_ref[...] * table[7:8]
    offset = jnp.sum(scaled * table[5:6], axis=1, keepdims=True)
    high, low = split2(scaled)
    both_ref[0:rows] = high
    both_ref[rows:] = low
    out_ref[...] = jnp.zeros_like(out_ref)

    def body(step, carry):
        dose = dose_ref[pl.ds(pl.multiple_of(step * TILE, TILE), TILE)]
        scores = matmul(both_ref[...], dose, NT)
        scores = scores[:rows] + scores[rows:] - carry
        pair = jnp.concatenate(split2(scores), axis=0)
        sums = matmul(pair, dose, NN)
        out_ref[...] += sums[:rows] + sums[rows:]
        return carry

    lax.fori_loop(0, dose_ref.shape[0] // TILE, body, offset)


def second_product(table, own, other, dose, mine):
    people, width = dose.shape
    rows = 2 * ROWS1
    return pl.pallas_call(
        functools.partial(second_kernel, mine=mine),
        in_specs=whole(4),
        out_specs=pl.BlockSpec(memory_space=pltpu.VMEM),
        out_shape=jax.ShapeDtypeStruct((rows, width), jnp.float32),
        scratch_shapes=[
            pltpu.VMEM((ROWS0, width), jnp.float32),
            pltpu.VMEM((rows, width), jnp.float32),
            pltpu.VMEM((2 * rows, width), jnp.bfloat16),
        ],
        compiler_params=params(),
        cost_estimate=pl.CostEstimate(
            flops=8 * people * width * rows, bytes_accessed=2 * people * width, transcendentals=0
        ),
    )(table, own, other, dose)


def finish_kernel(table_ref, own_ref, other_ref, mine_ref, got_ref, out_ref):
    core, place = here()
    half, width = own_ref.shape
    table = table_ref[:, lanes_of(place, 0, width)]
    row, fold_of, cutoff = base_rows(ROWS1)
    target = spread(table[:FOLDS], fold_of)
    coeff = soft_threshold(step_size * target, cutoff)
    scale = table[7:8] / PEOPLE
    low = jnp.where(core == 0, own_ref[...], other_ref[...])
    high = jnp.where(core == 0, other_ref[...], own_ref[...])
    old = jnp.concatenate([low, high], axis=0)[:ROWS1] * scale
    for group in range(2):
        shrink = shrink_unit * (2 * core + group + 1).astype(jnp.float32)
        new = next_coeff(coeff, old, target, shrink, cutoff)
        span = slice(group * ROWS1, (group + 1) * ROWS1)
        out_ref[span] = next_coeff(new, (mine_ref[span] + got_ref[span]) * scale, target, shrink, cutoff)


def finish(table, own, other, mine, got):
    return pl.pallas_call(
        finish_kernel,
        in_specs=whole(5),
        out_specs=pl.BlockSpec(memory_space=pltpu.VMEM),
        out_shape=jax.ShapeDtypeStruct(mine.shape, jnp.float32),
        compiler_params=params(),
    )(table, own, other, mine, got)


def predict_kernel(
    own_ref, other_ref, table_ref, fold_ref, dose_ref,
    coeff_out, number_out, score_out, coeff_ref, wide_ref, weight_ref, offset_ref,
):
    core, place = here()
    _, half, quarter = own_ref.shape
    width = dose_ref.shape[1]

    def order(first_ref, second_ref):
        for k in range(4):
            lanes = lanes_of(place, k, quarter)
            for part in range(quarter // 128):
                span = slice(part * 128, (part + 1) * 128)
                lane = (place ^ k) * (quarter // 128) + part
                coeff_ref[lane, 0:half] = first_ref[k, :, span]
                coeff_ref[lane, half:] = second_ref[k, :, span]
            for group in range(SHRINKS):
                ref = first_ref if group < 2 else second_ref
                start = group % 2 * ROWS1
                coeff_out[group * BASE : (group + 1) * BASE, lanes] = ref[k, start : start + BASE]

    @pl.when(core == 0)
    def _():
        order(own_ref, other_ref)

    @pl.when(core != 0)
    def _():
        order(other_ref, own_ref)

    for lane in range(width // 128):
        lanes = slice(lane * 128, (lane + 1) * 128)
        for fold in range(FOLDS):
            for group in range(SHRINKS):
                first = fold * LEVELS + group * LAMBDAS
                rows = pl.ds(group * ROWS1 + fold, LAMBDAS, FOLDS)
                wide_ref[first : first + LAMBDAS, lanes] = coeff_ref[lane, rows]
    table = table_ref[...]
    for fold in range(FOLDS):
        span = slice(fold * LEVELS, (fold + 1) * LEVELS)
        weighted = (wide_ref[span] * table[7:8]).astype(jnp.bfloat16)
        weight_ref[span] = weighted
        wide = weighted.astype(jnp.float32)
        offset_ref[span] = jnp.sum(wide * table[5:6], axis=1, keepdims=True)
        number_out[span] = jnp.sum(wide * table[8 + fold : 9 + fold], axis=1, keepdims=True)

    parts, _, tile = score_out.shape

    def body(part, carry):
        start = pl.multiple_of(part * tile, tile)
        scores = matmul(weight_ref[...], dose_ref[pl.ds(start, tile)], NT) - offset_ref[...]
        folds = fold_ref[:, pl.ds(start, tile)]
        out = scores[0:LEVELS]
        for fold in range(1, FOLDS):
            out = jnp.where(folds == fold, scores[fold * LEVELS : (fold + 1) * LEVELS], out)
        score_out[part] = out
        return carry

    lax.fori_loop(0, parts, body, 0)


def predict(own, other, table, fold_ids, dose, parts):
    people, width = dose.shape
    half = own.shape[1]
    return pl.pallas_call(
        predict_kernel,
        in_specs=whole(5),
        out_specs=whole(3),
        out_shape=[
            jax.ShapeDtypeStruct((GRID, width), jnp.float32),
            jax.ShapeDtypeStruct((GRID, 1), jnp.float32),
            jax.ShapeDtypeStruct((parts, LEVELS, people // parts), jnp.float32),
        ],
        scratch_shapes=[
            pltpu.VMEM((width // 128, 2 * half, 128), jnp.float32),
            pltpu.VMEM((GRID, width), jnp.float32),
            pltpu.VMEM((GRID, width), jnp.bfloat16),
            pltpu.VMEM((GRID, 1), jnp.float32),
        ],
        compiler_params=params(),
    )(own, other, table, fold_ids.reshape(1, people), dose)


def score_kernel(scores_ref, fold_ref, number_ref, out_ref):
    blocks, rows, people = scores_ref.shape
    start = pl.multiple_of(lax.axis_index("blk") * people, 128)
    folds = fold_ref[:, pl.ds(start, people)]
    scores = scores_ref[0]
    for block in range(1, blocks):
        scores = scores + scores_ref[block]
    square = scores * scores
    lane = lax.broadcasted_iota(jnp.int32, out_ref.shape, 1)
    out = jnp.zeros(out_ref.shape, jnp.float32)
    for fold in range(FOLDS):
        sums = jnp.sum(jnp.where(folds == fold, square, 0.0), axis=1, keepdims=True)
        out = jnp.where(lane == FOLDS + fold, sums, out)
        number = number_ref[fold * LEVELS : (fold + 1) * LEVELS] * (1.0 / lax.axis_size("samp"))
        out = jnp.where(lane == fold, number, out)
    out_ref[...] = out


def score_sums(scores, fold_ids, number):
    return pl.pallas_call(
        score_kernel,
        in_specs=whole(3),
        out_specs=pl.BlockSpec(memory_space=pltpu.VMEM),
        out_shape=jax.ShapeDtypeStruct((LEVELS, 128), jnp.float32),
        compiler_params=params(),
    )(scores, fold_ids.reshape(1, -1), number)


def local(genotypes, phenotype, fold_ids):
    dose, stats = prepare(genotypes, phenotype, fold_ids)
    stats = all_sum(stats, SAMP_BITS)

    kept, sent, table = first_product(stats, dose)
    piece = scatter_chips(kept, swap(sent, "samp", 1))
    own_product, other_product = gather_chips(piece + swap(piece, "samp", 8))

    sent = second_product(table, own_product, other_product, dose, False)
    sent = swap(sent, "samp", 1)
    kept = second_product(table, own_product, other_product, dose, True)
    piece = scatter_chips(kept, sent)
    piece = finish(table, own_product[0], other_product[0], piece, swap(piece, "samp", 8))
    own, other = gather_chips(piece)

    blocks = lax.axis_size("blk")
    coeff_all, numerator, scores = predict(own, other, table, fold_ids, dose, blocks)
    scores = lax.all_to_all(scores, "blk", 0, 0, tiled=True)
    sums = all_sum(score_sums(scores, fold_ids, numerator), ALL_BITS)
    counts = stats[7, :FOLDS]
    numerator = sums[:, :FOLDS] / (math.sqrt(SNPS) * counts)
    denominator = sums[:, FOLDS : 2 * FOLDS] / (SNPS * counts)
    fold_scores = jnp.stack([numerator.reshape(GRID), denominator.reshape(GRID)])
    return (coeff_all.T, fold_scores)


def solution(mesh):
    return jax.shard_map(
        local,
        mesh=mesh,
        in_specs=(P("samp", "blk"), P("samp"), P("samp")),
        out_specs=(P("blk", None), P()),
        check_vma=False,
    )
```

```python
import functools
import math

import jax
import jax.numpy as jnp
from jax import lax
from jax.experimental import pallas as pl
from jax.experimental.pallas import tpu as pltpu
from jax.sharding import PartitionSpec as P

FOLDS = 5
LAMBDAS = 20
GRID = 400
BASE = FOLDS * LAMBDAS
SHRINKS = GRID // BASE
LEVELS = GRID // FOLDS
ROWS0 = 112
ROWS1 = 104
PEOPLE = 32768
SNPS = 12288
TILE = 512

step_size = 0.6
epsilon = 1e-05
lambda_base = 0.1
lambda_ratio = 1.2
shrink_unit = 0.2

NT = (((1,), (1,)), ((), ()))
NN = (((1,), (0,)), ((), ()))
TN = (((0,), (0,)), ((), ()))


def matmul(left, right, dims):
    return lax.dot_general(left, right, dims, preferred_element_type=jnp.float32)


def soft_threshold(values, cutoff):
    return values - jnp.clip(values, -cutoff, cutoff)


def swap(values, axis, bit):
    size = lax.axis_size(axis)
    return lax.ppermute(values, axis, [(i, i ^ bit) for i in range(size)])


def split2(values):
    high = values.astype(jnp.bfloat16)
    return high, (values - high.astype(jnp.float32)).astype(jnp.bfloat16)


def all_sum(values, bits):
    for axis, group in bits:
        got = [swap(values, axis, bit) for bit in group]
        values = values + got[0] if len(got) == 1 else (values + got[0]) + (got[1] + got[2])
    return values


BOTH = ("samp", "blk")
SAMP_BITS = (("samp", (1,)), ("samp", (8,)), ("samp", (2, 4, 6)))
ALL_BITS = (("samp", (1,)), ("samp", (2, 4, 6)), ("blk", (1, 2, 3)), (BOTH, (4, 64, 68)))


def here():
    samp = lax.axis_index("samp")
    return samp & 1, (samp >> 1) & 3


def split_kernel(kept_ref, got_ref, *out_refs):
    width = out_refs[0].shape[1]
    place = here()[1]
    for k, out_ref in enumerate(out_refs):
        lanes = pl.ds(pl.multiple_of((place ^ k) * width, 128), width)
        out_ref[...] = kept_ref[:, lanes] + got_ref[:, lanes]


def scatter_chips(kept, got):
    rows, width = kept.shape
    mine, *sent = pl.pallas_call(
        split_kernel,
        in_specs=whole(2),
        out_specs=whole(4),
        out_shape=[jax.ShapeDtypeStruct((rows, width // 4), jnp.float32)] * 4,
        compiler_params=params(),
    )(kept, got)
    got = [swap(part, "samp", 2 * k) for k, part in zip((1, 2, 3), sent)]
    return (mine + got[0]) + (got[1] + got[2])


def gather_chips(piece):
    own = jnp.stack([piece] + [swap(piece, "samp", 2 * k) for k in (1, 2, 3)])
    return own, swap(own, "samp", 1)


def lanes_of(place, k, width):
    return pl.ds(pl.multiple_of((place ^ k) * width, 128), width)


def whole(count):
    return [pl.BlockSpec(memory_space=pltpu.VMEM)] * count


def params(mebibytes=20):
    return pltpu.CompilerParams(vmem_limit_bytes=mebibytes * 1024 * 1024)


def parts3(values):
    high, rest = split2(values)
    rest = values - high.astype(jnp.float32)
    mid, low = split2(rest)
    return [part.astype(jnp.float32) for part in (high, mid, low)]


def prepare_kernel(pheno_ref, fold_ref, geno_ref, dose_ref, stats_ref, buffer_ref, left_ref, sums_ref, sems):
    people, width = dose_ref.shape
    parts = sems.shape[0]
    tile = people // parts
    copies = [
        pltpu.make_async_copy(
            geno_ref.at[pl.ds(part * tile, tile)], buffer_ref.at[pl.ds(part * tile, tile)], sems.at[part]
        )
        for part in range(parts)
    ]
    for copy in copies:
        copy.start()
    line = lax.broadcasted_iota(jnp.int32, (8, people), 0)
    chosen = line == fold_ref[...]
    split = jnp.where(chosen, pheno_ref[...], 0.0)
    high, mid, low = parts3(split)
    high = jnp.where(line == FOLDS, 1.0, high)
    left_ref[...] = jnp.concatenate([high, mid, low, jnp.zeros_like(low)], axis=0).astype(jnp.bfloat16)
    counts = jnp.sum(chosen.astype(jnp.float32), axis=1, keepdims=True)
    sums = jnp.sum(split, axis=1, keepdims=True)
    lane = lax.broadcasted_iota(jnp.int32, (1, width), 1)
    extra = jnp.zeros((1, width), jnp.float32)
    for fold in range(FOLDS):
        extra = jnp.where(lane == fold, counts[fold : fold + 1], extra)
        extra = jnp.where(lane == FOLDS + fold, sums[fold : fold + 1], extra)
    squares = jnp.zeros((8, width), jnp.float32)
    for part in range(parts):
        copies[part].wait()
        span = slice(part * tile, (part + 1) * tile)
        values = buffer_ref[span].astype(jnp.float32)
        dose = values.astype(jnp.bfloat16)
        dose_ref[span] = dose
        product = matmul(left_ref[:, span], dose, NN)
        sums_ref[...] = product if part == 0 else sums_ref[...] + product
        squares += jnp.sum((values * values).reshape(-1, 8, width), axis=0)
    stats_ref[0:8] = sums_ref[0:8] + sums_ref[8:16] + sums_ref[16:24]
    stats_ref[6:7] = jnp.sum(squares, axis=0, keepdims=True)
    stats_ref[7:8] = extra


def prepare(genotypes, phenotype, fold_ids, parts=8):
    people, width = genotypes.shape
    return pl.pallas_call(
        prepare_kernel,
        in_specs=whole(2) + [pl.BlockSpec(memory_space=pl.ANY)],
        out_specs=whole(2),
        out_shape=[
            jax.ShapeDtypeStruct((people, width), jnp.bfloat16),
            jax.ShapeDtypeStruct((8, width), jnp.float32),
        ],
        scratch_shapes=[
            pltpu.VMEM((people, width), jnp.int32),
            pltpu.VMEM((32, people), jnp.bfloat16),
            pltpu.VMEM((32, width), jnp.float32),
            pltpu.SemaphoreType.DMA((parts,)),
        ],
        compiler_params=params(36),
    )(phenotype.reshape(1, people), fold_ids.reshape(1, people), genotypes)


def base_rows(rows):
    row = lax.broadcasted_iota(jnp.int32, (rows, 1), 0)
    cutoff = step_size * (lambda_base * jnp.exp((row // FOLDS).astype(jnp.float32) * math.log(lambda_ratio)))
    return row, row % FOLDS, cutoff


def spread(table, fold_of):
    out = jnp.broadcast_to(table[FOLDS - 1 : FOLDS], (fold_of.shape[0], table.shape[1]))
    for fold in range(FOLDS - 1):
        out = jnp.where(fold_of == fold, table[fold : fold + 1], out)
    return out


def next_coeff(coeff, product, target, shrink, cutoff):
    gradient = (1.0 - shrink) * product + shrink * coeff - target
    return soft_threshold(coeff - step_size * gradient, cutoff)


def first_kernel(stats_ref, dose_ref, kept_ref, sent_ref, table_ref, both_ref, total_ref):
    stats = stats_ref[...]
    mean = stats[5:6] / PEOPLE
    scales = jnp.sqrt(stats[6:7] / PEOPLE - mean * mean + epsilon)
    inverse = 1.0 / scales
    lane = lax.broadcasted_iota(jnp.int32, (1, stats.shape[1]), 1)
    pick = lambda place: jnp.sum(jnp.where(lane == place, stats[7:8], 0.0), axis=1, keepdims=True)
    counts = [pick(fold) for fold in range(FOLDS)]
    sums = [pick(FOLDS + fold) for fold in range(FOLDS)]
    every = sums[0] + sums[1] + sums[2] + sums[3] + sums[4]
    geno_pheno = jnp.sum(stats[0:FOLDS], axis=0, keepdims=True)
    row, fold_of, cutoff = base_rows(ROWS0)
    target = jnp.zeros((ROWS0, stats.shape[1]), jnp.float32)
    for fold in range(FOLDS):
        train = geno_pheno - stats[fold : fold + 1]
        zscore = (train - (every - sums[fold]) * mean) / (scales * jnp.sqrt(PEOPLE - counts[fold]))
        table_ref[fold : fold + 1] = zscore
        table_ref[8 + fold : 9 + fold] = stats[fold : fold + 1] - mean * sums[fold]
        target = jnp.where(fold_of == fold, zscore, target)
    table_ref[5:6] = mean
    table_ref[6:7] = scales
    table_ref[7:8] = inverse
    table_ref[13:16] = jnp.zeros((3, stats.shape[1]), jnp.float32)
    coeff = soft_threshold(step_size * target, cutoff)
    scaled = jnp.where(row < BASE, coeff * inverse, 0.0)
    high, low = split2(scaled)
    both_ref[...] = jnp.zeros_like(both_ref)
    both_ref[0:ROWS0] = high
    both_ref[128 : 128 + ROWS0] = low
    line = lax.broadcasted_iota(jnp.int32, (16, 1), 0)
    mean_high, mean_mid, mean_low = parts3(mean)
    means = jnp.where(line == 0, mean_high, jnp.where(line == 1, mean_mid, jnp.where(line == 2, mean_low, 0.0)))
    offset = jnp.sum(matmul(means.astype(jnp.bfloat16), both_ref[...], NT), axis=0, keepdims=True)
    offset = offset[:, :128] + offset[:, 128:]
    total_ref[...] = jnp.zeros_like(total_ref)

    def body(step, carry):
        dose = dose_ref[pl.ds(pl.multiple_of(step * TILE, TILE), TILE)]
        scores = matmul(dose, both_ref[...], NT)
        scores = scores[:, :128] + scores[:, 128:] - carry
        pair = jnp.concatenate(split2(scores), axis=1)
        total_ref[...] += matmul(pair, dose, TN)
        return carry

    lax.fori_loop(0, dose_ref.shape[0] // TILE, body, offset)
    half = ROWS0 // 2
    first = total_ref[0:half] + total_ref[128 : 128 + half]
    second = total_ref[half:ROWS0] + total_ref[128 + half : 128 + ROWS0]
    is_first = here()[0] == 0
    kept_ref[...] = jnp.where(is_first, first, second)
    sent_ref[...] = jnp.where(is_first, second, first)


def first_product(stats, dose):
    width = dose.shape[1]
    half = jax.ShapeDtypeStruct((ROWS0 // 2, width), jnp.float32)
    return pl.pallas_call(
        first_kernel,
        in_specs=whole(2),
        out_specs=whole(3),
        out_shape=[half, half, jax.ShapeDtypeStruct((16, width), jnp.float32)],
        scratch_shapes=[pltpu.VMEM((256, width), jnp.bfloat16), pltpu.VMEM((256, width), jnp.float32)],
        compiler_params=params(),
    )(stats, dose)


def gram_kernel(dose_ref, *out_refs, mine):
    core, place = here()
    side = core if mine else 1 - core
    rows, width = out_refs[0].shape
    step = 256
    for block in range(rows // step):
        left = dose_ref[:, pl.ds(pl.multiple_of(side * rows + block * step, 128), step)].T
        for k, out_ref in enumerate(out_refs):
            right = dose_ref[:, lanes_of(place, k, width)]
            out_ref[block * step : (block + 1) * step] = matmul(left, right, NN)


def gram_parts(dose, mine):
    people, width = dose.shape
    part = jax.ShapeDtypeStruct((width // 2, width // 4), jnp.float32)
    return pl.pallas_call(
        functools.partial(gram_kernel, mine=mine),
        in_specs=whole(1),
        out_specs=whole(4),
        out_shape=[part] * 4,
        compiler_params=params(16),
        cost_estimate=pl.CostEstimate(
            flops=people * width * width, bytes_accessed=2 * people * width, transcendentals=0
        ),
    )(dose)


def second_kernel(
    table_ref, own_ref, other_ref, g0_ref, g1_ref, g2_ref, g3_ref,
    kept_ref, sent_ref, product_ref, coeff_ref, both_ref, gram_ref,
):
    core, place = here()
    half, width = own_ref.shape[1:]
    rows = coeff_ref.shape[0]
    for part in range(2):
        k = place ^ (2 * core + part)
        lanes = slice(part * width, (part + 1) * width)
        own, other = own_ref[k], other_ref[k]
        product_ref[0:half, lanes] = jnp.where(core == 0, own, other)
        product_ref[half:, lanes] = jnp.where(core == 0, other, own)
    table = table_ref[:, pl.ds(pl.multiple_of(core * 2 * width, 128), 2 * width)]
    row, fold_of, cutoff = base_rows(ROWS1)
    target = spread(table[:FOLDS], fold_of)
    coeff = soft_threshold(step_size * target, cutoff)
    product = product_ref[0:ROWS1] * (table[7:8] / PEOPLE)
    for group in range(SHRINKS):
        new = next_coeff(coeff, product, target, shrink_unit * (group + 1), cutoff)
        coeff_ref[group * ROWS1 : (group + 1) * ROWS1] = jnp.where(row < BASE, new, 0.0)
    high, low = split2(coeff_ref[...] * table[7:8])
    both_ref[0:rows] = high
    both_ref[rows:] = low
    scaled = high.astype(jnp.float32) + low.astype(jnp.float32)
    offset = jnp.sum(scaled * table[5:6], axis=1, keepdims=True)
    gram = (g0_ref[...] + g1_ref[...]) + (g2_ref[...] + g3_ref[...])
    high, low = split2(gram)
    gram_ref[:, :width] = high
    gram_ref[:, width:] = low
    sums = matmul(both_ref[...], gram_ref[...], NN)
    sums = sums[:rows] + sums[rows:]
    mean = table_ref[5:6, lanes_of(place, 0, width)]
    sums = sums[:, :width] + sums[:, width:] - (0.5 * PEOPLE) * offset * mean
    kept_ref[...] = jnp.where(core == 0, sums[: rows // 2], sums[rows // 2 :])
    sent_ref[...] = jnp.where(core == 0, sums[rows // 2 :], sums[: rows // 2])


def second_product(table, own, other, panels):
    depth, width = panels[0].shape
    half = jax.ShapeDtypeStruct((2 * ROWS1, width), jnp.float32)
    return pl.pallas_call(
        second_kernel,
        in_specs=whole(7),
        out_specs=whole(2),
        out_shape=[half, half],
        scratch_shapes=[
            pltpu.VMEM((ROWS0, depth), jnp.float32),
            pltpu.VMEM((4 * ROWS1, depth), jnp.float32),
            pltpu.VMEM((8 * ROWS1, depth), jnp.bfloat16),
            pltpu.VMEM((depth, 2 * width), jnp.bfloat16),
        ],
        compiler_params=params(28),
    )(table, own, other, *panels)


def finish_kernel(table_ref, own_ref, other_ref, mine_ref, got_ref, out_ref):
    core, place = here()
    half, width = own_ref.shape
    table = table_ref[:, lanes_of(place, 0, width)]
    row, fold_of, cutoff = base_rows(ROWS1)
    target = spread(table[:FOLDS], fold_of)
    coeff = soft_threshold(step_size * target, cutoff)
    scale = table[7:8] / PEOPLE
    low = jnp.where(core == 0, own_ref[...], other_ref[...])
    high = jnp.where(core == 0, other_ref[...], own_ref[...])
    old = jnp.concatenate([low, high], axis=0)[:ROWS1] * scale
    for group in range(2):
        shrink = shrink_unit * (2 * core + group + 1).astype(jnp.float32)
        new = next_coeff(coeff, old, target, shrink, cutoff)
        span = slice(group * ROWS1, (group + 1) * ROWS1)
        out_ref[span] = next_coeff(new, (mine_ref[span] + got_ref[span]) * scale, target, shrink, cutoff)


def finish(table, own, other, mine, got):
    return pl.pallas_call(
        finish_kernel,
        in_specs=whole(5),
        out_specs=pl.BlockSpec(memory_space=pltpu.VMEM),
        out_shape=jax.ShapeDtypeStruct(mine.shape, jnp.float32),
        compiler_params=params(),
    )(table, own, other, mine, got)


def predict_kernel(
    own_ref, other_ref, table_ref, fold_ref, dose_ref,
    coeff_out, number_out, score_out, coeff_ref, wide_ref, weight_ref, offset_ref,
):
    core, place = here()
    _, half, quarter = own_ref.shape
    width = dose_ref.shape[1]

    def order(first_ref, second_ref):
        for k in range(4):
            lanes = lanes_of(place, k, quarter)
            for part in range(quarter // 128):
                span = slice(part * 128, (part + 1) * 128)
                lane = (place ^ k) * (quarter // 128) + part
                coeff_ref[lane, 0:half] = first_ref[k, :, span]
                coeff_ref[lane, half:] = second_ref[k, :, span]
            for group in range(SHRINKS):
                ref = first_ref if group < 2 else second_ref
                start = group % 2 * ROWS1
                coeff_out[group * BASE : (group + 1) * BASE, lanes] = ref[k, start : start + BASE]

    @pl.when(core == 0)
    def _():
        order(own_ref, other_ref)

    @pl.when(core != 0)
    def _():
        order(other_ref, own_ref)

    for lane in range(width // 128):
        lanes = slice(lane * 128, (lane + 1) * 128)
        for fold in range(FOLDS):
            for group in range(SHRINKS):
                first = fold * LEVELS + group * LAMBDAS
                rows = pl.ds(group * ROWS1 + fold, LAMBDAS, FOLDS)
                wide_ref[first : first + LAMBDAS, lanes] = coeff_ref[lane, rows]
    table = table_ref[...]
    for fold in range(FOLDS):
        span = slice(fold * LEVELS, (fold + 1) * LEVELS)
        weighted = (wide_ref[span] * table[7:8]).astype(jnp.bfloat16)
        weight_ref[span] = weighted
        wide = weighted.astype(jnp.float32)
        offset_ref[span] = jnp.sum(wide * table[5:6], axis=1, keepdims=True)
        number_out[span] = jnp.sum(wide * table[8 + fold : 9 + fold], axis=1, keepdims=True)

    parts, _, tile = score_out.shape

    def body(part, carry):
        start = pl.multiple_of(part * tile, tile)
        scores = matmul(weight_ref[...], dose_ref[pl.ds(start, tile)], NT) - offset_ref[...]
        folds = fold_ref[:, pl.ds(start, tile)]
        out = scores[0:LEVELS]
        for fold in range(1, FOLDS):
            out = jnp.where(folds == fold, scores[fold * LEVELS : (fold + 1) * LEVELS], out)
        score_out[part] = out
        return carry

    lax.fori_loop(0, parts, body, 0)


def predict(own, other, table, fold_ids, dose, parts):
    people, width = dose.shape
    half = own.shape[1]
    return pl.pallas_call(
        predict_kernel,
        in_specs=whole(5),
        out_specs=whole(3),
        out_shape=[
            jax.ShapeDtypeStruct((GRID, width), jnp.float32),
            jax.ShapeDtypeStruct((GRID, 1), jnp.float32),
            jax.ShapeDtypeStruct((parts, LEVELS, people // parts), jnp.float32),
        ],
        scratch_shapes=[
            pltpu.VMEM((width // 128, 2 * half, 128), jnp.float32),
            pltpu.VMEM((GRID, width), jnp.float32),
            pltpu.VMEM((GRID, width), jnp.bfloat16),
            pltpu.VMEM((GRID, 1), jnp.float32),
        ],
        compiler_params=params(28),
    )(own, other, table, fold_ids.reshape(1, people), dose)


def score_kernel(scores_ref, fold_ref, number_ref, out_ref):
    blocks, rows, people = scores_ref.shape
    start = pl.multiple_of(lax.axis_index("blk") * people, 128)
    folds = fold_ref[:, pl.ds(start, people)]
    scores = scores_ref[0]
    for block in range(1, blocks):
        scores = scores + scores_ref[block]
    square = scores * scores
    lane = lax.broadcasted_iota(jnp.int32, out_ref.shape, 1)
    out = jnp.zeros(out_ref.shape, jnp.float32)
    for fold in range(FOLDS):
        sums = jnp.sum(jnp.where(folds == fold, square, 0.0), axis=1, keepdims=True)
        out = jnp.where(lane == FOLDS + fold, sums, out)
        number = number_ref[fold * LEVELS : (fold + 1) * LEVELS] * (1.0 / lax.axis_size("samp"))
        out = jnp.where(lane == fold, number, out)
    out_ref[...] = out


def score_sums(scores, fold_ids, number):
    return pl.pallas_call(
        score_kernel,
        in_specs=whole(3),
        out_specs=pl.BlockSpec(memory_space=pltpu.VMEM),
        out_shape=jax.ShapeDtypeStruct((LEVELS, 128), jnp.float32),
        compiler_params=params(),
    )(scores, fold_ids.reshape(1, -1), number)


def local(genotypes, phenotype, fold_ids):
    dose, stats = prepare(genotypes, phenotype, fold_ids)
    stats = all_sum(stats, SAMP_BITS)

    got = [swap(part, "samp", 1) for part in gram_parts(dose, False)]
    parts = [a + b for a, b in zip(gram_parts(dose, True), got)]
    panels = [parts[0]] + [swap(parts[k], "samp", 2 * k) for k in (1, 2, 3)]

    kept, sent, table = first_product(stats, dose)
    piece = scatter_chips(kept, swap(sent, "samp", 1))
    own_product, other_product = gather_chips(piece + swap(piece, "samp", 8))

    kept, sent = second_product(table, own_product, other_product, panels)
    piece = kept + swap(sent, "samp", 1)
    piece = finish(table, own_product[0], other_product[0], piece, swap(piece, "samp", 8))
    own, other = gather_chips(piece)

    blocks = lax.axis_size("blk")
    coeff_all, numerator, scores = predict(own, other, table, fold_ids, dose, blocks)
    scores = lax.all_to_all(scores, "blk", 0, 0, tiled=True)
    sums = all_sum(score_sums(scores, fold_ids, numerator), ALL_BITS)
    counts = stats[7, :FOLDS]
    numerator = sums[:, :FOLDS] / (math.sqrt(SNPS) * counts)
    denominator = sums[:, FOLDS : 2 * FOLDS] / (SNPS * counts)
    fold_scores = jnp.stack([numerator.reshape(GRID), denominator.reshape(GRID)])
    return (coeff_all.T, fold_scores)


def solution(mesh):
    return jax.shard_map(
        local,
        mesh=mesh,
        in_specs=(P("samp", "blk"), P("samp"), P("samp")),
        out_specs=(P("blk", None), P()),
        check_vma=False,
    )
```
